32 devices in a mesh: gx: 4 (over z), gy: 4 (over y, core), gz: 2 (over x).
Axes of the slice: x: 2, y: 2, z: 4, core: 2. Of those that a mesh axis runs over, the one named last changes fastest.
Arguments:
- tokens: bfloat16 [32, 32, 16, 384], P('gx', 'gy', 'gz'), may hold values from -60 to 60
- frozen: int32 [32, 32, 16], P('gx', 'gy', 'gz'), may hold values 0 or 1
- cotangent: bfloat16 [32, 32, 16, 384], P('gx', 'gy', 'gz'), may hold values from -6 to 6
- w_qkv: bfloat16 [384, 1152], replicated, may hold values from -0.3125 to 0.3125
- w_proj: bfloat16 [384, 384], replicated, may hold values from -0.3125 to 0.3125
- norm_gain: float32 [384], replicated, may hold values from 0.5 to 8
Outputs:
- block_out: bfloat16 [32, 32, 16, 384], P('gx', 'gy', 'gz')
- tokens_grad: bfloat16 [32, 32, 16, 384], P('gx', 'gy', 'gz')
- qkv_grad: float32 [384, 1152], replicated
- proj_grad: float32 [384, 384], replicated
- gain_grad: float32 [384], replicated
The draws below stay inside these ranges and needn't reach their ends.
All inputs are finite; a program needn't handle non-finite values. No bound on the sum of `frozen` on one device may be relied on, other than what follows from the above.
Results may differ from the reference program's by a relative error of at most 0.015.
The reference program's roundings to bfloat16 on the way count: a program that leaves them out, or rounds other values in their place, can miss the bound.
Values may be sent and summed in bfloat16 or wider, within the bound.
A program may use at most 64 MiB of HBM per device.

```python
import math
import jax
import jax.numpy as jnp
from jax import lax

D = 384
HEADS = 12
HDIM = 32
WIN = 8
NX = 32
NY = 32
NZ = 16


def draw_tokens(key, part):
    key = jax.random.fold_in(key, 11)
    key_base, key_scale = jax.random.split(key, 2)
    shape_all = (NX, NY, NZ, D)
    base_draw = jnp.clip(jax.random.normal(key_base, shape_all, jnp.float32), -6.0, 6.0)
    row_scale = jnp.exp(jax.random.uniform(key_scale, (NX, NY, NZ, 1), jnp.float32, 0.0, math.log(10.0)))
    return jnp.clip(base_draw * row_scale, -60.0, 60.0).astype(jnp.bfloat16)


def draw_norm_gain(key, part):
    key = jax.random.fold_in(key, 12)
    return jax.random.uniform(key, (D,), jnp.float32, 0.5, 2.0)


def place_ends(values, own_key, smallest, top_value):
    longest = values.shape.index(max(values.shape))
    spots = []
    for shift in (0, 1):
        where = [jax.random.randint(jax.random.fold_in(own_key, axis), (), 0, length) for axis, length in enumerate(values.shape)]
        where[longest] = (where[longest] + shift) % values.shape[longest]
        spots.append(tuple(where))
    return values.at[spots[0]].set(smallest).at[spots[1]].set(top_value)


def block_levels(key, shape, pieces, smallest, top_value):
    level = 1.0
    for axis_at, blocks in pieces:
        draws = jax.random.uniform(jax.random.fold_in(jax.random.fold_in(key, 6), axis_at), (blocks,), jnp.float32, smallest / len(pieces), top_value / len(pieces))
        level = level * jnp.repeat(jnp.exp(draws), shape[axis_at] // blocks).reshape((-1,) + (1,) * (len(shape) - 1 - axis_at))
    return level


def gaussian(key, extent, deviation, limit, cuts=(), kind=jnp.bfloat16):
    drawn = jax.random.normal(key, extent, jnp.float32) * deviation
    if len(cuts) > 0:
        drawn = block_levels(key, extent, cuts, -0.22, 0.18) * drawn
    return jnp.clip(drawn, min=-limit, max=limit).astype(kind)


def setup_inputs(seed: int = 0) -> dict:
    splits = jax.random.split(jax.random.key(seed), 7)
    tokens = draw_tokens(jax.random.fold_in(splits[6], 71), 0)
    frozen = place_ends((jax.random.randint(splits[1], (NX, NY, NZ), 0, 2) < 1).astype(jnp.int32), jax.random.fold_in(splits[1], 1), 0, 1)
    cotangent = gaussian(splits[2], (NX, NY, NZ, D), 1.0, 6.0, ((0, 4), (1, 4), (2, 2)))
    w_qkv = gaussian(splits[3], (D, 3 * D), D ** -0.5, 0.3125)
    w_proj = gaussian(splits[4], (D, D), D ** -0.5, 0.3125)
    norm_gain = draw_norm_gain(jax.random.fold_in(splits[6], 71), 0)
    return dict(tokens=tokens, frozen=frozen, cotangent=cotangent, w_qkv=w_qkv, w_proj=w_proj, norm_gain=norm_gain)


EPSILON = 1e-05

def head_pass(queries, key_rows, values, d_mixed):
    score_scale = HDIM ** (-0.5)
    scores = jnp.dot(queries, key_rows.T, preferred_element_type=jnp.float32) * score_scale
    top_score = lax.optimization_barrier(jnp.max(scores, axis=-1, keepdims=True))
    exp_terms = jnp.exp(scores - top_score)
    attn_probs = exp_terms / lax.optimization_barrier(jnp.sum(exp_terms, axis=-1, keepdims=True))
    probs_low = attn_probs.astype(jnp.bfloat16)
    mixed_head = jnp.dot(probs_low, values, preferred_element_type=jnp.float32).astype(jnp.bfloat16)
    d_values = jnp.dot(probs_low.T, d_mixed, preferred_element_type=jnp.float32).astype(jnp.bfloat16)
    d_probs = jnp.dot(d_mixed, values.T, preferred_element_type=jnp.float32)
    d_scores = (attn_probs * (d_probs - lax.optimization_barrier(jnp.sum(attn_probs * d_probs, axis=-1, keepdims=True))) * score_scale).astype(jnp.bfloat16)
    d_queries = jnp.dot(d_scores, key_rows, preferred_element_type=jnp.float32).astype(jnp.bfloat16)
    d_keys = jnp.dot(d_scores.T, queries, preferred_element_type=jnp.float32).astype(jnp.bfloat16)
    return (mixed_head, d_queries, d_keys, d_values)

def split_heads(rows):
    return rows.reshape(rows.shape[0], HEADS, HDIM).transpose(1, 0, 2)

def join_heads(heads_rows):
    return heads_rows.transpose(1, 0, 2).reshape(heads_rows.shape[1], HEADS * HDIM)

def window_pass(window_rows, window_cot, w_qkv, w_proj, norm_gain):
    widened = window_rows.astype(jnp.float32)
    row_mean = lax.optimization_barrier(jnp.mean(widened, axis=-1, keepdims=True))
    centred = widened - row_mean
    inv_std = lax.rsqrt(lax.optimization_barrier(jnp.mean(centred * centred, axis=-1, keepdims=True)) + EPSILON)
    unit_rows = centred * inv_std
    normed = (unit_rows * norm_gain).astype(jnp.bfloat16)
    qkv_rows = jnp.dot(normed, w_qkv, preferred_element_type=jnp.float32).astype(jnp.bfloat16)
    d_mixed = jnp.dot(window_cot, w_proj.T, preferred_element_type=jnp.float32).astype(jnp.bfloat16)
    heads_out = lax.map(lambda grouped: head_pass(*grouped), (split_heads(qkv_rows[:, :D]), split_heads(qkv_rows[:, D:2 * D]), split_heads(qkv_rows[:, 2 * D:]), split_heads(d_mixed)))
    mixed_rows = join_heads(heads_out[0])
    branch = jnp.dot(mixed_rows, w_proj, preferred_element_type=jnp.float32).astype(jnp.bfloat16)
    d_qkv = jnp.concatenate([join_heads(heads_out[1]), join_heads(heads_out[2]), join_heads(heads_out[3])], axis=1)
    proj_term = jnp.dot(mixed_rows.T, window_cot, preferred_element_type=jnp.float32)
    qkv_term = jnp.dot(normed.T, d_qkv, preferred_element_type=jnp.float32)
    d_normed = jnp.dot(d_qkv, w_qkv.T, preferred_element_type=jnp.float32)
    gain_term = lax.optimization_barrier(jnp.sum(d_normed * unit_rows, axis=0))
    scaled_grad = d_normed * norm_gain
    d_rows = (inv_std * (scaled_grad - lax.optimization_barrier(jnp.mean(scaled_grad, axis=-1, keepdims=True)) - unit_rows * lax.optimization_barrier(jnp.mean(scaled_grad * unit_rows, axis=-1, keepdims=True)))).astype(jnp.bfloat16)
    return (branch, d_rows, qkv_term, proj_term, gain_term)

def partition(block):
    first, second, third, width = block.shape
    grid = block.reshape(first // WIN, WIN, second // WIN, WIN, third // WIN, WIN, width)
    return grid.transpose(0, 2, 4, 1, 3, 5, 6).reshape(-1, WIN ** 3, width)

def assemble(windows, first, second, third):
    grid = windows.reshape(first // WIN, second // WIN, third // WIN, WIN, WIN, WIN, windows.shape[-1])
    return grid.transpose(0, 3, 1, 4, 2, 5, 6).reshape(first, second, third, windows.shape[-1])

def reference(tokens, frozen, cotangent, w_qkv, w_proj, norm_gain):
    kept = jnp.where(frozen[..., None] == 1, tokens, jnp.zeros_like(tokens))
    half_width = WIN // 2
    shifted = jnp.roll(kept, (-half_width, -half_width, -half_width), axis=(0, 1, 2))
    shifted_cot = jnp.roll(cotangent, (-half_width, -half_width, -half_width), axis=(0, 1, 2))
    zeros_init = (jnp.zeros((D, 3 * D), jnp.float32), jnp.zeros((D, D), jnp.float32), jnp.zeros((D,), jnp.float32))

    def window_step(totals, window_pair):
        results = window_pass(window_pair[0], window_pair[1], w_qkv, w_proj, norm_gain)
        return ((totals[0] + results[2], totals[1] + results[3], totals[2] + results[4]), (results[0], results[1]))
    totals, blocks = lax.scan(window_step, zeros_init, (partition(shifted), partition(shifted_cot)))
    branch = jnp.roll(assemble(blocks[0], NX, NY, NZ), (half_width, half_width, half_width), axis=(0, 1, 2))
    d_rows = jnp.roll(assemble(blocks[1], NX, NY, NZ), (half_width, half_width, half_width), axis=(0, 1, 2))
    block_out = (kept.astype(jnp.float32) + branch.astype(jnp.float32)).astype(jnp.bfloat16)
    tokens_grad = jnp.where(frozen[..., None] == 1, cotangent.astype(jnp.float32) + d_rows.astype(jnp.float32), jnp.zeros((), jnp.float32)).astype(jnp.bfloat16)
    grad_scale = (NX * NY * NZ) ** (-0.5)
    return (block_out, tokens_grad, totals[0] * grad_scale, totals[1] * grad_scale, totals[2] * grad_scale)
```

```python
import functools

import jax
import jax.numpy as jnp
from jax import lax
from jax.experimental import pallas as pl
from jax.experimental.pallas import tpu as pltpu
from jax.sharding import PartitionSpec as P

D = 384
HEADS = 12
HDIM = 32
WIN = 8
HALF = WIN // 2
OCT = HALF**3
ROWS = WIN**3
LANES = 128
PER_GROUP = LANES // HDIM
GROUPS = D // LANES
GRAD_ROWS = 4 * GROUPS * D
PARTS = 3
EPSILON = 1e-05
SCALE = HDIM ** (-0.5)
LOG2E = 1.4426950408889634
AXES = ("gx", "gy", "gz")
MESH = pl.DeviceIdType.MESH
VMEM_LIMIT = 56 * 1024 * 1024

OCTANTS = [(k // 4, k // 2 % 2, k % 2) for k in range(8)]


def neighbour(octant, direction):
    place = []
    for bit, axis in zip(octant, AXES, strict=True):
        size = lax.axis_size(axis)
        at = lax.axis_index(axis)
        place.append(at if bit else lax.rem(at + size + direction, size))
    return tuple(place)


def stages():
    found = []
    for axis in ("gy", "gz", "gx"):
        step = 1
        while step < lax.axis_size(axis):
            found.append((axis, step))
            step *= 2
    return found


def my_bit(axis, step):
    return lax.rem(lax.axis_index(axis) // step, 2)


def partner(axis, step):
    place = []
    for name in AXES:
        at = lax.axis_index(name)
        place.append(at + step * (1 - 2 * my_bit(axis, step)) if name == axis else at)
    return tuple(place)


def part_plan(order):
    plan, held = [], GRAD_ROWS // PARTS
    for axis, step in order:
        halved = held % 32 == 0
        if halved:
            held //= 2
        plan.append((axis, step, held, halved))
    return plan


def exchange_kernel(block_ref, window_ref, send_sem, recv_sem, own_sem):
    barrier = pltpu.get_barrier_semaphore()
    for octant in OCTANTS[:7]:
        pl.semaphore_signal(barrier, inc=1, device_id=neighbour(octant, 1), device_id_type=MESH)
    own = pltpu.make_async_copy(block_ref.at[7], window_ref.at[7], own_sem)
    own.start()
    pl.semaphore_wait(barrier, 7)
    copies = []
    for k, octant in enumerate(OCTANTS[:7]):
        copy = pltpu.make_async_remote_copy(
            src_ref=block_ref.at[k],
            dst_ref=window_ref.at[k],
            send_sem=send_sem.at[k],
            recv_sem=recv_sem.at[k],
            device_id=neighbour(octant, -1),
            device_id_type=MESH,
        )
        copy.start()
        copies.append(copy)
    own.wait()
    for copy in copies:
        copy.wait()


def dot(a, b):
    return lax.dot_general(a, b, (((1,), (0,)), ((), ())), preferred_element_type=jnp.float32)


def dot_nt(a, b):
    return lax.dot_general(a, b, (((1,), (1,)), ((), ())), preferred_element_type=jnp.float32)


def window_kernel(
    window_ref,
    w_qkv_ref,
    w_proj_ref,
    gain_ref,
    back_ref,
    grad_ref,
    gain_grad_ref,
    unit,
    inv_std,
    normed,
    qkv,
    d_mixed,
    d_qkv,
    mixed_t,
):
    rows = window_ref[:, :D].astype(jnp.float32)
    centred = rows - jnp.mean(rows, axis=-1, keepdims=True)
    inv = lax.rsqrt(jnp.mean(centred * centred, axis=-1, keepdims=True) + EPSILON)
    inv_std[...] = inv
    unit_rows = centred * inv
    unit[...] = unit_rows
    normed[...] = (unit_rows * gain_ref[...]).astype(jnp.bfloat16)
    qkv[...] = dot(normed[...], w_qkv_ref[...]).astype(jnp.bfloat16)
    d_mixed[...] = dot_nt(window_ref[:, D:], w_proj_ref[...]).astype(jnp.bfloat16)

    lane = lax.broadcasted_iota(jnp.int32, (ROWS, LANES), 1)

    def group(g, carry):
        at = [pl.ds(pl.multiple_of(part * D + g * LANES, LANES), LANES) for part in range(3)]
        queries, key_rows, values = (qkv[:, where] for where in at)
        cot = d_mixed[:, at[0]]
        keys_t = key_rows.T
        values_t = values.T
        d_keys = jnp.zeros((ROWS, LANES), jnp.float32)
        d_values = jnp.zeros((ROWS, LANES), jnp.float32)
        d_queries_t = []
        mixed_parts = []
        for h in range(PER_GROUP):
            mine = (lane >= h * HDIM) & (lane < (h + 1) * HDIM)
            own_queries = jnp.where(mine, queries, jnp.zeros_like(queries))
            own_cot = jnp.where(mine, cot, jnp.zeros_like(cot))
            head = slice(h * HDIM, (h + 1) * HDIM)
            scores = dot_nt(key_rows, own_queries)
            top = jnp.max(scores, axis=0, keepdims=True)
            exp_terms = jnp.exp2((scores - top) * (SCALE * LOG2E))
            probs = exp_terms * (1.0 / jnp.sum(exp_terms, axis=0, keepdims=True))
            probs_low = probs.astype(jnp.bfloat16)
            mixed_parts.append(dot(values_t[head], probs_low).astype(jnp.bfloat16))
            d_values += dot(probs_low, own_cot)
            d_probs = dot_nt(values, own_cot)
            total = jnp.sum(probs * d_probs, axis=0, keepdims=True)
            d_scores = (probs * (d_probs - total) * SCALE).astype(jnp.bfloat16)
            d_queries_t.append(dot(keys_t[head], d_scores).astype(jnp.bfloat16))
            d_keys += dot(d_scores, own_queries)
        mixed_t[at[0], :] = jnp.concatenate(mixed_parts, axis=0)
        d_qkv[:, at[0]] = jnp.concatenate(d_queries_t, axis=0).T
        d_qkv[:, at[1]] = d_keys.astype(jnp.bfloat16)
        d_qkv[:, at[2]] = d_values.astype(jnp.bfloat16)
        return carry

    lax.fori_loop(0, GROUPS, group, 0)

    back_ref[:, :D] = dot(mixed_t[...].T, w_proj_ref[...]).astype(jnp.bfloat16)
    normed_t = normed[...].T
    for j in range(3 * GROUPS):
        grad_ref[j * D : (j + 1) * D, :] = dot(normed_t, d_qkv[:, j * LANES : (j + 1) * LANES])
    for j in range(GROUPS):
        start = (3 * GROUPS + j) * D
        grad_ref[start : start + D, :] = dot(
            mixed_t[...], window_ref[:, D + j * LANES : D + (j + 1) * LANES]
        )
    d_normed = dot_nt(d_qkv[...], w_qkv_ref[...])
    unit_rows = unit[...]
    gain_term = jnp.sum(d_normed * unit_rows, axis=0, keepdims=True)
    gain_grad_ref[...] = jnp.zeros_like(gain_grad_ref)
    for j in range(GROUPS):
        gain_grad_ref[j : j + 1, :] = gain_term[:, j * LANES : (j + 1) * LANES]
    scaled = d_normed * gain_ref[...]
    back_ref[:, D:] = (
        inv_std[...]
        * (
            scaled
            - jnp.mean(scaled, axis=-1, keepdims=True)
            - unit_rows * jnp.mean(scaled * unit_rows, axis=-1, keepdims=True)
        )
    ).astype(jnp.bfloat16)


def return_kernel(
    order,
    back_ref,
    grad_ref,
    gain_ref,
    restored_ref,
    total_ref,
    gain_total_ref,
    acc,
    landing,
    gain_landing,
    back_send,
    back_recv,
    own_sem,
    reduce_send,
    reduce_recv,
    gather_send,
    gather_recv,
    gain_send,
    gain_recv,
):
    count = len(order)
    barrier = pltpu.get_barrier_semaphore()
    for octant in OCTANTS[:7]:
        pl.semaphore_signal(barrier, inc=1, device_id=neighbour(octant, -1), device_id_type=MESH)
    for axis, step in order:
        pl.semaphore_signal(barrier, inc=1, device_id=partner(axis, step), device_id_type=MESH)
    own = pltpu.make_async_copy(back_ref.at[7], restored_ref.at[7], own_sem)
    own.start()
    pl.semaphore_wait(barrier, 7 + count)

    plans = [part_plan(order[:1] + order[1 + p :] + order[1 : 1 + p]) for p in range(PARTS)]
    base = GRAD_ROWS // PARTS
    low = [jnp.int32(p * base) for p in range(PARTS)]
    pending = []

    def send_terms(p, s):
        axis, step, rows, halved = plans[p][s]
        bit = my_bit(axis, step)
        offset = p * landing.shape[0] // PARTS + sum(entry[2] for entry in plans[p][:s])
        start = low[p] + (1 - bit) * rows if halved else low[p]
        source = grad_ref if s == 0 else acc
        copy = pltpu.make_async_remote_copy(
            src_ref=source.at[pl.ds(pl.multiple_of(start, 16), rows)],
            dst_ref=landing.at[pl.ds(offset, rows)],
            send_sem=reduce_send.at[p, s],
            recv_sem=reduce_recv.at[p, s],
            device_id=partner(axis, step),
            device_id_type=MESH,
        )
        copy.start()
        keep = low[p] + bit * rows if halved else low[p]
        return copy, keep, offset, rows, halved

    def send_gain(s):
        axis, step = order[s]
        copy = pltpu.make_async_remote_copy(
            src_ref=gain_ref if s == 0 else gain_total_ref,
            dst_ref=gain_landing.at[s],
            send_sem=gain_send.at[s],
            recv_sem=gain_recv.at[s],
            device_id=partner(axis, step),
            device_id_type=MESH,
        )
        copy.start()
        return copy

    for s in range(count):
        started = [send_terms(p, s) for p in range(PARTS)]
        gain_copy = send_gain(s)
        if s == 0:
            backs = []
            for k, octant in enumerate(OCTANTS[:7]):
                copy = pltpu.make_async_remote_copy(
                    src_ref=back_ref.at[k],
                    dst_ref=restored_ref.at[k],
                    send_sem=back_send.at[k],
                    recv_sem=back_recv.at[k],
                    device_id=neighbour(octant, 1),
                    device_id_type=MESH,
                )
                copy.start()
                backs.append(copy)
        for p, (copy, keep, offset, rows, halved) in enumerate(started):
            source = grad_ref if s == 0 else acc
            copy.wait_recv()
            if halved:
                pending.append(copy)
            else:
                copy.wait_send()
            where = pl.ds(pl.multiple_of(keep, 16), rows)
            acc[where, :] = source[where, :] + landing[offset : offset + rows, :]
            low[p] = keep
        gain_copy.wait()
        previous = gain_ref if s == 0 else gain_total_ref
        gain_total_ref[...] = previous[...] + gain_landing[s]

    for p in range(PARTS):
        where = pl.ds(pl.multiple_of(low[p], 16), plans[p][-1][2])
        total_ref[where, :] = acc[where, :].astype(jnp.bfloat16)

    for s in reversed(range(count)):
        gathers = []
        for p in range(PARTS):
            axis, step, rows, halved = plans[p][s]
            if not halved:
                continue
            where = pl.ds(pl.multiple_of(low[p], 16), rows)
            copy = pltpu.make_async_remote_copy(
                src_ref=total_ref.at[where],
                dst_ref=total_ref.at[where],
                send_sem=gather_send.at[p, s],
                recv_sem=gather_recv.at[p, s],
                device_id=partner(axis, step),
                device_id_type=MESH,
            )
            copy.start()
            gathers.append(copy)
            low[p] = low[p] - my_bit(axis, step) * rows
        for copy in gathers:
            copy.wait_recv()
            pending.append(copy)

    for copy in pending:
        copy.wait_send()
    own.wait()
    for copy in backs:
        copy.wait()


def in_vmem(count):
    return [pl.BlockSpec(memory_space=pltpu.VMEM)] * count


def exchange(block):
    return pl.pallas_call(
        exchange_kernel,
        out_shape=jax.ShapeDtypeStruct(block.shape, block.dtype),
        in_specs=in_vmem(1),
        out_specs=in_vmem(1)[0],
        scratch_shapes=[
            pltpu.SemaphoreType.DMA((7,)),
            pltpu.SemaphoreType.DMA((7,)),
            pltpu.SemaphoreType.DMA,
        ],
        compiler_params=pltpu.CompilerParams(
            collective_id=0, has_side_effects=True, vmem_limit_bytes=VMEM_LIMIT
        ),
    )(block)


def window_pass(window, w_qkv, w_proj, norm_gain):
    low, wide = jnp.bfloat16, jnp.float32
    return pl.pallas_call(
        window_kernel,
        out_shape=(
            jax.ShapeDtypeStruct((ROWS, 2 * D), low),
            jax.ShapeDtypeStruct((GRAD_ROWS, LANES), wide),
            jax.ShapeDtypeStruct((8, LANES), wide),
        ),
        in_specs=in_vmem(4),
        out_specs=tuple(in_vmem(3)),
        scratch_shapes=[
            pltpu.VMEM((ROWS, D), wide),
            pltpu.VMEM((ROWS, 1), wide),
            pltpu.VMEM((ROWS, D), low),
            pltpu.VMEM((ROWS, 3 * D), low),
            pltpu.VMEM((ROWS, D), low),
            pltpu.VMEM((ROWS, 3 * D), low),
            pltpu.VMEM((D, ROWS), low),
        ],
        compiler_params=pltpu.CompilerParams(vmem_limit_bytes=VMEM_LIMIT),
    )(window, w_qkv, w_proj, norm_gain)


def send_back(back, grad, gain):
    order = stages()
    count = len(order)
    landing_rows = PARTS * sum(entry[2] for entry in part_plan(order))
    dma = pltpu.SemaphoreType.DMA
    return pl.pallas_call(
        functools.partial(return_kernel, order),
        out_shape=(
            jax.ShapeDtypeStruct(back.shape, back.dtype),
            jax.ShapeDtypeStruct(grad.shape, jnp.bfloat16),
            jax.ShapeDtypeStruct(gain.shape, gain.dtype),
        ),
        in_specs=in_vmem(3),
        out_specs=tuple(in_vmem(3)),
        scratch_shapes=[
            pltpu.VMEM(grad.shape, jnp.float32),
            pltpu.VMEM((landing_rows, LANES), jnp.float32),
            pltpu.VMEM((count, *gain.shape), jnp.float32),
            dma((7,)),
            dma((7,)),
            dma,
            dma((PARTS, count)),
            dma((PARTS, count)),
            dma((PARTS, count)),
            dma((PARTS, count)),
            dma((count,)),
            dma((count,)),
        ],
        compiler_params=pltpu.CompilerParams(
            collective_id=1, has_side_effects=True, vmem_limit_bytes=VMEM_LIMIT
        ),
    )(back, grad, gain)


def local(tokens, frozen, cotangent, w_qkv, w_proj, norm_gain):
    mask = frozen[..., None] == 1
    kept = jnp.where(mask, tokens, jnp.zeros_like(tokens))
    block = jnp.concatenate([kept, cotangent], axis=-1)
    block = block.reshape(2, HALF, 2, HALF, 2, HALF, 2 * D).transpose(0, 2, 4, 1, 3, 5, 6)
    window = exchange(block.reshape(8, OCT, 2 * D)).reshape(ROWS, 2 * D)
    back, grad, gain = window_pass(window, w_qkv, w_proj, norm_gain.reshape(1, D))
    restored, grad, gain = send_back(back.reshape(8, OCT, 2 * D), grad, gain)
    restored = restored.reshape(2, 2, 2, HALF, HALF, HALF, 2 * D).transpose(0, 3, 1, 4, 2, 5, 6)
    restored = restored.reshape(WIN, WIN, WIN, 2 * D).astype(jnp.float32)
    block_out = (kept.astype(jnp.float32) + restored[..., :D]).astype(jnp.bfloat16)
    tokens_grad = jnp.where(
        mask, cotangent.astype(jnp.float32) + restored[..., D:], jnp.zeros((), jnp.float32)
    ).astype(jnp.bfloat16)
    everyone = ROWS
    for axis in AXES:
        everyone *= lax.axis_size(axis)
    grad_scale = everyone ** (-0.5)
    grad = grad.reshape(4 * GROUPS, D, LANES).astype(jnp.float32) * grad_scale
    qkv_grad = grad[: 3 * GROUPS].transpose(1, 0, 2).reshape(D, 3 * D)
    proj_grad = grad[3 * GROUPS :].transpose(1, 0, 2).reshape(D, D)
    return (block_out, tokens_grad, qkv_grad, proj_grad, gain[:GROUPS].reshape(D) * grad_scale)


def solution(mesh):
    lattice = P(*AXES, None)
    return jax.shard_map(
        local,
        mesh=mesh,
        in_specs=(lattice, P(*AXES), lattice, P(), P(), P()),
        out_specs=(lattice, lattice, P(), P(), P()),
        check_vma=False,
    )
```

```python
import functools

import jax
import jax.numpy as jnp
from jax import lax
from jax.experimental import pallas as pl
from jax.experimental.pallas import tpu as pltpu
from jax.sharding import PartitionSpec as P

D = 384
HEADS = 12
HDIM = 32
WIN = 8
HALF = WIN // 2
OCT = HALF**3
ROWS = WIN**3
LANES = 128
PER_GROUP = LANES // HDIM
GROUPS = D // LANES
GRAD_ROWS = 4 * GROUPS * D
PARTS = 3
EPSILON = 1e-05
SCALE = HDIM ** (-0.5)
LOG2E = 1.4426950408889634
AXES = ("gx", "gy", "gz")
MESH = pl.DeviceIdType.MESH
VMEM_LIMIT = 56 * 1024 * 1024

OCTANTS = [
    (1, 1, 1),
    (1, 1, 0),
    (1, 0, 1),
    (0, 1, 1),
    (1, 0, 0),
    (0, 1, 0),
    (0, 0, 1),
    (0, 0, 0),
]


def neighbour(octant, direction):
    place = []
    for bit, axis in zip(octant, AXES, strict=True):
        size = lax.axis_size(axis)
        at = lax.axis_index(axis)
        place.append(at if bit else lax.rem(at + size + direction, size))
    return tuple(place)


def stages():
    bits = []
    for axis in ("gy", "gz", "gx"):
        step = 1
        while step < lax.axis_size(axis):
            bits.append((axis, step))
            step *= 2
    return [bits[:1]] + [bits[i : i + 2] for i in range(1, len(bits), 2)]


def my_bit(axis, step):
    return lax.rem(lax.axis_index(axis) // step, 2)


def partner(bits, flips):
    place = {axis: lax.axis_index(axis) for axis in AXES}
    digit = 0
    for i, (axis, step) in enumerate(bits):
        bit = my_bit(axis, step)
        if flips >> i & 1:
            place[axis] = place[axis] + step * (1 - 2 * bit)
            bit = 1 - bit
        digit = digit + bit * 2**i
    return tuple(place[axis] for axis in AXES), digit


def plan_stages(order):
    plan, held = [], GRAD_ROWS // PARTS
    for bits in order:
        count = 2 ** len(bits)
        divided = held % (16 * count) == 0
        if divided:
            held //= count
        plan.append((bits, held, divided))
    return plan


def tree_sum(terms):
    while len(terms) > 1:
        terms = [a + b for a, b in zip(terms[::2], terms[1::2], strict=True)]
    return terms[0]


def remote(src, dst, send_sem, recv_sem, device):
    copy = pltpu.make_async_remote_copy(
        src_ref=src,
        dst_ref=dst,
        send_sem=send_sem,
        recv_sem=recv_sem,
        device_id=device,
        device_id_type=MESH,
    )
    copy.start()
    return copy


def reduce_part(plan, p, grad, landing, total_ref, sems, unsent):
    reduce_send, reduce_recv, gather_send, gather_recv = sems
    low = p * (GRAD_ROWS // PARTS)
    offset = p * (landing.shape[0] // PARTS)
    for s, (bits, rows, divided) in enumerate(plan):
        copies = []
        for flips in range(1, 2 ** len(bits)):
            device, digit = partner(bits, flips)
            start = pl.multiple_of(low + digit * rows, 16) if divided else low
            copies.append(
                remote(
                    grad.at[pl.ds(start, rows)],
                    landing.at[pl.ds(offset + (flips - 1) * rows, rows)],
                    reduce_send.at[p, s, flips - 1],
                    reduce_recv.at[p, s, flips - 1],
                    device,
                )
            )
        yield
        for copy in copies:
            copy.wait_recv()
            if divided:
                unsent.append(copy)
            else:
                copy.wait_send()
        if divided:
            low = pl.multiple_of(low + partner(bits, 0)[1] * rows, 16)
        where = pl.ds(low, rows)
        terms = [grad[where, :]]
        for _ in copies:
            terms.append(landing[offset : offset + rows, :])
            offset += rows
        grad[where, :] = tree_sum(terms)
    where = pl.ds(low, plan[-1][1])
    total_ref[where, :] = grad[where, :].astype(jnp.bfloat16)
    for s, (bits, rows, divided) in reversed(list(enumerate(plan))):
        if not divided:
            continue
        copies = []
        where = pl.ds(low, rows)
        for flips in range(1, 2 ** len(bits)):
            copies.append(
                remote(
                    total_ref.at[where],
                    total_ref.at[where],
                    gather_send.at[p, s, flips - 1],
                    gather_recv.at[p, s, flips - 1],
                    partner(bits, flips)[0],
                )
            )
        yield
        for copy in copies:
            copy.wait_recv()
            unsent.append(copy)
        low = pl.multiple_of(low - partner(bits, 0)[1] * rows, 16)


def reduce_gain(order, gain_ref, landing, send_sem, recv_sem):
    for s, bits in enumerate(order):
        copies = []
        for flips in range(1, 2 ** len(bits)):
            copies.append(
                remote(
                    gain_ref,
                    landing.at[s, flips - 1],
                    send_sem.at[s, flips - 1],
                    recv_sem.at[s, flips - 1],
                    partner(bits, flips)[0],
                )
            )
        yield
        for copy in copies:
            copy.wait()
        terms = [gain_ref[...]] + [landing[s, i] for i in range(len(copies))]
        gain_ref[...] = tree_sum(terms)


def dot(a, b):
    return lax.dot_general(a, b, (((1,), (0,)), ((), ())), preferred_element_type=jnp.float32)


def dot_nt(a, b):
    return lax.dot_general(a, b, (((1,), (1,)), ((), ())), preferred_element_type=jnp.float32)


def split_octants(block):
    pairs = block.reshape(HALF, 2, WIN, WIN, D)
    even, odd = pairs[:, 0], pairs[:, 1]
    first = lax.broadcasted_iota(jnp.int32, even.shape, 2) < HALF
    halves = [
        jnp.where(first, even, swapped(odd)),
        jnp.where(first, swapped(even), odd),
    ]
    found = []
    for ox, oy, oz in OCTANTS:
        part = halves[oz][2 * ox : 2 * ox + 2, HALF * oy : HALF * oy + HALF]
        found.append(part.reshape(OCT, D))
    return found


def join_octants(octants):
    parts = dict(zip(OCTANTS, octants, strict=True))
    halves = []
    for oz in range(2):
        rows = []
        for ox in range(2):
            both = [parts[ox, oy, oz].reshape(2, HALF, WIN, D) for oy in range(2)]
            rows.append(jnp.concatenate(both, axis=1))
        halves.append(jnp.concatenate(rows, axis=0))
    lower, upper = halves
    first = lax.broadcasted_iota(jnp.int32, lower.shape, 2) < HALF
    even = jnp.where(first, lower, swapped(upper))
    odd = jnp.where(first, swapped(lower), upper)
    return jnp.stack([even, odd], axis=1).reshape(WIN, WIN, WIN, D)


def swapped(rows):
    shape = rows.shape
    return pltpu.roll(rows.reshape(-1, WIN, D), HALF, 1).reshape(shape)


def kept_tokens(tokens_ref, frozen_ref):
    mask = jnp.broadcast_to(frozen_ref[...], (WIN, WIN, WIN, D)) == 1
    return mask, jnp.where(mask, tokens_ref[...].astype(jnp.float32), 0.0)


def main_kernel(
    order,
    tokens_ref,
    frozen_ref,
    cot_ref,
    w_qkv_ref,
    w_proj_ref,
    gain_ref,
    restored_ref,
    total_ref,
    gain_total_ref,
    block,
    window,
    unit,
    inv_std,
    normed,
    qkv,
    d_mixed,
    d_qkv,
    mixed_t,
    back,
    grad,
    landing,
    gain_landing,
    out_send,
    out_recv,
    back_send,
    back_recv,
    reduce_send,
    reduce_recv,
    gather_send,
    gather_recv,
    gain_send,
    gain_recv,
):
    barrier = pltpu.get_barrier_semaphore()
    greeted = 0
    for octant in OCTANTS[1:]:
        for direction in (-1, 1):
            device = neighbour(octant, direction)
            pl.semaphore_signal(barrier, inc=1, device_id=device, device_id_type=MESH)
            greeted += 1
    for bits in order:
        for flips in range(1, 2 ** len(bits)):
            device = partner(bits, flips)[0]
            pl.semaphore_signal(barrier, inc=1, device_id=device, device_id_type=MESH)
            greeted += 1

    kept = split_octants(kept_tokens(tokens_ref, frozen_ref)[1])
    cot = split_octants(cot_ref[...].astype(jnp.float32))
    for k in range(8):
        target = block.at[k] if k else window.at[0:OCT]
        target[:, :D] = kept[k].astype(jnp.bfloat16)
        target[:, D:] = cot[k].astype(jnp.bfloat16)
    pl.semaphore_wait(barrier, greeted)
    unsent = []
    arriving = [None]
    for k in range(1, 8):
        device = neighbour(OCTANTS[k], -1)
        where = pl.ds(k * OCT, OCT)
        arriving.append(
            remote(block.at[k], window.at[where], out_send.at[k - 1], out_recv.at[k - 1], device)
        )

    half_rows = ROWS // 2
    for part in range(2):
        for copy in arriving[4 * part : 4 * part + 4]:
            if copy is not None:
                copy.wait_recv()
                unsent.append(copy)
        at = slice(part * half_rows, (part + 1) * half_rows)
        rows = window[at, :D].astype(jnp.float32)
        centred = rows - jnp.mean(rows, axis=-1, keepdims=True)
        inv = lax.rsqrt(jnp.mean(centred * centred, axis=-1, keepdims=True) + EPSILON)
        inv_std[at, :] = inv
        unit_part = centred * inv
        unit[at, :] = unit_part
        normed_part = (unit_part * gain_ref[...]).astype(jnp.bfloat16)
        normed[at, :] = normed_part
        qkv[at, :] = dot(normed_part, w_qkv_ref[...]).astype(jnp.bfloat16)
        d_mixed[at, :] = dot_nt(window[at, D:], w_proj_ref[...]).astype(jnp.bfloat16)

    plan = plan_stages(order)
    sems = (reduce_send, reduce_recv, gather_send, gather_recv)
    running = []

    def advance():
        for task in list(running):
            if next(task, "done") == "done":
                running.remove(task)

    def launch(task):
        next(task)
        running.append(task)

    lane = lax.broadcasted_iota(jnp.int32, (ROWS, LANES), 1)
    normed_t = normed[...].T
    window_cot = window[:, D:]

    for g in range(GROUPS):
        at = [slice(part * D + g * LANES, part * D + (g + 1) * LANES) for part in range(3)]
        queries, key_rows, values = (qkv[:, where] for where in at)
        cot_rows = d_mixed[:, at[0]]
        keys_t = key_rows.T
        values_t = values.T
        d_keys = jnp.zeros((ROWS, LANES), jnp.float32)
        d_values = jnp.zeros((ROWS, LANES), jnp.float32)
        d_queries_t = []
        mixed_parts = []
        for h in range(PER_GROUP):
            mine = (lane >= h * HDIM) & (lane < (h + 1) * HDIM)
            own_queries = jnp.where(mine, queries, jnp.zeros_like(queries))
            own_cot = jnp.where(mine, cot_rows, jnp.zeros_like(cot_rows))
            head = slice(h * HDIM, (h + 1) * HDIM)
            scores = dot_nt(key_rows, own_queries)
            top = jnp.max(scores, axis=0, keepdims=True)
            exp_terms = jnp.exp2((scores - top) * (SCALE * LOG2E))
            probs = exp_terms * (1.0 / jnp.sum(exp_terms, axis=0, keepdims=True))
            probs_low = probs.astype(jnp.bfloat16)
            mixed_parts.append(dot(values_t[head], probs_low).astype(jnp.bfloat16))
            d_values += dot(probs_low, own_cot)
            d_probs = dot_nt(values, own_cot)
            total = jnp.sum(probs * d_probs, axis=0, keepdims=True)
            d_scores = (probs * (d_probs - total) * SCALE).astype(jnp.bfloat16)
            d_queries_t.append(dot(keys_t[head], d_scores).astype(jnp.bfloat16))
            d_keys += dot(d_scores, own_queries)
        mixed_t[at[0], :] = jnp.concatenate(mixed_parts, axis=0)
        d_qkv[:, at[0]] = jnp.concatenate(d_queries_t, axis=0).T
        d_qkv[:, at[1]] = d_keys.astype(jnp.bfloat16)
        d_qkv[:, at[2]] = d_values.astype(jnp.bfloat16)
        start = g * (GRAD_ROWS // PARTS)
        for part in range(3):
            grad[start : start + D, :] = dot(normed_t, d_qkv[:, at[part]])
            start += D
        proj_term = dot(mixed_t[at[0], :], window_cot)
        for j in range(GROUPS):
            grad[start : start + LANES, :] = proj_term[:, j * LANES : (j + 1) * LANES]
            start += LANES
        advance()
        launch(reduce_part(plan, g, grad, landing, total_ref, sems, unsent))

    def send_back(which):
        for k in range(1, 8):
            copy = remote(
                back.at[which, k],
                restored_ref.at[which, k],
                back_send.at[which, k - 1],
                back_recv.at[which, k - 1],
                neighbour(OCTANTS[k], 1),
            )
            unsent.append(copy)
            returning.append(copy)

    returning = []
    branch = dot(mixed_t[...].T, w_proj_ref[...]).astype(jnp.bfloat16)
    back[0] = branch.reshape(8, OCT, D)
    send_back(0)
    advance()
    d_normed = dot_nt(d_qkv[...], w_qkv_ref[...])
    unit_rows = unit[...]
    gain_term = jnp.sum(d_normed * unit_rows, axis=0, keepdims=True)
    gain_total_ref[...] = jnp.zeros_like(gain_total_ref)
    for j in range(GROUPS):
        gain_total_ref[j : j + 1, :] = gain_term[:, j * LANES : (j + 1) * LANES]
    launch(reduce_gain(order, gain_total_ref, gain_landing, gain_send, gain_recv))
    scaled = d_normed * gain_ref[...]
    d_rows = (
        inv_std[...]
        * (
            scaled
            - jnp.mean(scaled, axis=-1, keepdims=True)
            - unit_rows * jnp.mean(scaled * unit_rows, axis=-1, keepdims=True)
        )
    ).astype(jnp.bfloat16)
    back[1] = d_rows.reshape(8, OCT, D)
    send_back(1)
    for which in range(2):
        restored_ref[which, 0] = back[which, 0]
    while running:
        advance()
    for copy in returning:
        copy.wait_recv()
    for copy in unsent:
        copy.wait_send()


def finish_kernel(
    scale,
    tokens_ref,
    frozen_ref,
    cot_ref,
    restored_ref,
    total_ref,
    gain_total_ref,
    out_ref,
    tokens_grad_ref,
    qkv_grad_ref,
    proj_grad_ref,
    gain_grad_ref,
):
    wide = jnp.float32
    mask, kept = kept_tokens(tokens_ref, frozen_ref)
    branch = join_octants([restored_ref[0, k].astype(wide) for k in range(8)])
    out_ref[...] = (kept + branch).astype(jnp.bfloat16)
    d_rows = join_octants([restored_ref[1, k].astype(wide) for k in range(8)])
    both = cot_ref[...].astype(wide) + d_rows
    tokens_grad_ref[...] = jnp.where(mask, both, 0.0).astype(jnp.bfloat16)
    start = 0
    for g in range(GROUPS):
        for part in range(3):
            column = part * D + g * LANES
            qkv_grad_ref[:, column : column + LANES] = total_ref[start : start + D, :].astype(wide) * scale
            start += D
        for j in range(GROUPS):
            proj_grad_ref[g * LANES : (g + 1) * LANES, j * LANES : (j + 1) * LANES] = (
                total_ref[start : start + LANES, :].astype(wide) * scale
            )
            start += LANES
    gain_grad_ref[...] = gain_total_ref[...] * scale


def in_vmem(count):
    return [pl.BlockSpec(memory_space=pltpu.VMEM)] * count


def local(tokens, frozen, cotangent, w_qkv, w_proj, norm_gain):
    low, wide = jnp.bfloat16, jnp.float32
    shape = jax.ShapeDtypeStruct
    frozen = frozen[..., None]
    order = stages()
    count = len(order)
    landing_rows = PARTS * sum(
        (2 ** len(bits) - 1) * rows for bits, rows, _ in plan_stages(order)
    )
    dma = pltpu.SemaphoreType.DMA
    restored, total, gain = pl.pallas_call(
        functools.partial(main_kernel, order),
        out_shape=(
            shape((2, 8, OCT, D), low),
            shape((GRAD_ROWS, LANES), low),
            shape((8, LANES), wide),
        ),
        in_specs=in_vmem(6),
        out_specs=tuple(in_vmem(3)),
        scratch_shapes=[
            pltpu.VMEM((8, OCT, 2 * D), low),
            pltpu.VMEM((ROWS, 2 * D), low),
            pltpu.VMEM((ROWS, D), wide),
            pltpu.VMEM((ROWS, 1), wide),
            pltpu.VMEM((ROWS, D), low),
            pltpu.VMEM((ROWS, 3 * D), low),
            pltpu.VMEM((ROWS, D), low),
            pltpu.VMEM((ROWS, 3 * D), low),
            pltpu.VMEM((D, ROWS), low),
            pltpu.VMEM((2, 8, OCT, D), low),
            pltpu.VMEM((GRAD_ROWS, LANES), wide),
            pltpu.VMEM((landing_rows, LANES), wide),
            pltpu.VMEM((count, 3, 8, LANES), wide),
            dma((7,)),
            dma((7,)),
            dma((2, 7)),
            dma((2, 7)),
            dma((PARTS, count, 3)),
            dma((PARTS, count, 3)),
            dma((PARTS, count, 3)),
            dma((PARTS, count, 3)),
            dma((count, 3)),
            dma((count, 3)),
        ],
        compiler_params=pltpu.CompilerParams(
            collective_id=0, has_side_effects=True, vmem_limit_bytes=VMEM_LIMIT
        ),
    )(tokens, frozen, cotangent, w_qkv, w_proj, norm_gain.reshape(1, D))
    everyone = ROWS
    for axis in AXES:
        everyone *= lax.axis_size(axis)
    block_out, tokens_grad, qkv_grad, proj_grad, gain = pl.pallas_call(
        functools.partial(finish_kernel, everyone ** (-0.5)),
        out_shape=(
            shape(tokens.shape, low),
            shape(tokens.shape, low),
            shape((D, 3 * D), wide),
            shape((D, D), wide),
            shape((8, LANES), wide),
        ),
        in_specs=in_vmem(6),
        out_specs=tuple(in_vmem(5)),
        compiler_params=pltpu.CompilerParams(vmem_limit_bytes=VMEM_LIMIT),
    )(tokens, frozen, cotangent, restored, total, gain)
    return (block_out, tokens_grad, qkv_grad, proj_grad, gain[:GROUPS].reshape(D))


def solution(mesh):
    lattice = P(*AXES, None)
    return jax.shard_map(
        local,
        mesh=mesh,
        in_specs=(lattice, P(*AXES), lattice, P(), P(), P()),
        out_specs=(lattice, lattice, P(), P(), P()),
        check_vma=False,
    )
```

```python
import functools

import jax
import jax.numpy as jnp
from jax import lax
from jax.experimental import pallas as pl
from jax.experimental.pallas import tpu as pltpu
from jax.sharding import PartitionSpec as P

D = 384
HEADS = 12
HDIM = 32
WIN = 8
HALF = WIN // 2
OCT = HALF**3
ROWS = WIN**3
LANES = 128
PER_GROUP = LANES // HDIM
GROUPS = D // LANES
GRAD_ROWS = 4 * GROUPS * D
PARTS = 3
EPSILON = 1e-05
SCALE = HDIM ** (-0.5)
LOG2E = 1.4426950408889634
AXES = ("gx", "gy", "gz")
MESH = pl.DeviceIdType.MESH
VMEM_LIMIT = 56 * 1024 * 1024

OCTANTS = [
    (1, 1, 1),
    (1, 1, 0),
    (1, 0, 1),
    (0, 1, 1),
    (1, 0, 0),
    (0, 1, 0),
    (0, 0, 1),
    (0, 0, 0),
]


def neighbour(octant, direction):
    place = []
    for bit, axis in zip(octant, AXES, strict=True):
        size = lax.axis_size(axis)
        at = lax.axis_index(axis)
        place.append(at if bit else lax.rem(at + size + direction, size))
    return tuple(place)


def stages():
    bits = []
    for axis in ("gy", "gz", "gx"):
        step = 1
        while step < lax.axis_size(axis):
            bits.append((axis, step))
            step *= 2
    return [bits[:1]] + [bits[i : i + 2] for i in range(1, len(bits), 2)]


def my_bit(axis, step):
    return lax.rem(lax.axis_index(axis) // step, 2)


def partner(bits, flips):
    place = {axis: lax.axis_index(axis) for axis in AXES}
    digit = 0
    for i, (axis, step) in enumerate(bits):
        bit = my_bit(axis, step)
        if flips >> i & 1:
            place[axis] = place[axis] + step * (1 - 2 * bit)
            bit = 1 - bit
        digit = digit + bit * 2**i
    return tuple(place[axis] for axis in AXES), digit


def plan_stages(order):
    plan, held = [], GRAD_ROWS // PARTS
    for bits in order:
        count = 2 ** len(bits)
        divided = held % (16 * count) == 0
        if divided:
            held //= count
        plan.append((bits, held, divided))
    return plan


def tree_sum(terms):
    while len(terms) > 1:
        terms = [a + b for a, b in zip(terms[::2], terms[1::2], strict=True)]
    return terms[0]


def remote(src, dst, send_sem, recv_sem, device):
    copy = pltpu.make_async_remote_copy(
        src_ref=src,
        dst_ref=dst,
        send_sem=send_sem,
        recv_sem=recv_sem,
        device_id=device,
        device_id_type=MESH,
    )
    copy.start()
    return copy


def reduce_part(plan, p, grad, landing, total_ref, sems, unsent):
    reduce_send, reduce_recv, gather_send, gather_recv = sems
    low = p * (GRAD_ROWS // PARTS)
    offset = p * (landing.shape[0] // PARTS)
    for s, (bits, rows, divided) in enumerate(plan):
        copies = []
        for flips in range(1, 2 ** len(bits)):
            device, digit = partner(bits, flips)
            start = pl.multiple_of(low + digit * rows, 16) if divided else low
            copies.append(
                remote(
                    grad.at[pl.ds(start, rows)],
                    landing.at[pl.ds(offset + (flips - 1) * rows, rows)],
                    reduce_send.at[p, s, flips - 1],
                    reduce_recv.at[p, s, flips - 1],
                    device,
                )
            )
        yield
        for copy in copies:
            copy.wait_recv()
            if divided:
                unsent.append(copy)
            else:
                copy.wait_send()
        if divided:
            low = pl.multiple_of(low + partner(bits, 0)[1] * rows, 16)
        where = pl.ds(low, rows)
        terms = [grad[where, :]]
        for _ in copies:
            terms.append(landing[offset : offset + rows, :])
            offset += rows
        grad[where, :] = tree_sum(terms)
    where = pl.ds(low, plan[-1][1])
    total_ref[where, :] = grad[where, :].astype(jnp.bfloat16)
    for s, (bits, rows, divided) in reversed(list(enumerate(plan))):
        if not divided:
            continue
        copies = []
        where = pl.ds(low, rows)
        for flips in range(1, 2 ** len(bits)):
            copies.append(
                remote(
                    total_ref.at[where],
                    total_ref.at[where],
                    gather_send.at[p, s, flips - 1],
                    gather_recv.at[p, s, flips - 1],
                    partner(bits, flips)[0],
                )
            )
        yield
        for copy in copies:
            copy.wait_recv()
            unsent.append(copy)
        low = pl.multiple_of(low - partner(bits, 0)[1] * rows, 16)


def reduce_gain(order, gain_ref, landing, send_sem, recv_sem):
    for s, bits in enumerate(order):
        copies = []
        for flips in range(1, 2 ** len(bits)):
            copies.append(
                remote(
                    gain_ref,
                    landing.at[s, flips - 1],
                    send_sem.at[s, flips - 1],
                    recv_sem.at[s, flips - 1],
                    partner(bits, flips)[0],
                )
            )
        yield
        for copy in copies:
            copy.wait()
        terms = [gain_ref[...]] + [landing[s, i] for i in range(len(copies))]
        gain_ref[...] = tree_sum(terms)


def dot(a, b):
    return lax.dot_general(a, b, (((1,), (0,)), ((), ())), preferred_element_type=jnp.float32)


def dot_nt(a, b):
    return lax.dot_general(a, b, (((1,), (1,)), ((), ())), preferred_element_type=jnp.float32)


def split_octants(block):
    pairs = block.reshape(HALF, 2, WIN, WIN, D)
    even, odd = pairs[:, 0], pairs[:, 1]
    first = lax.broadcasted_iota(jnp.int32, even.shape, 2) < HALF
    halves = [
        jnp.where(first, even, swapped(odd)),
        jnp.where(first, swapped(even), odd),
    ]
    found = []
    for ox, oy, oz in OCTANTS:
        part = halves[oz][2 * ox : 2 * ox + 2, HALF * oy : HALF * oy + HALF]
        found.append(part.reshape(OCT, D))
    return found


def join_octants(octants):
    parts = dict(zip(OCTANTS, octants, strict=True))
    halves = []
    for oz in range(2):
        rows = []
        for ox in range(2):
            both = [parts[ox, oy, oz].reshape(2, HALF, WIN, D) for oy in range(2)]
            rows.append(jnp.concatenate(both, axis=1))
        halves.append(jnp.concatenate(rows, axis=0))
    lower, upper = halves
    first = lax.broadcasted_iota(jnp.int32, lower.shape, 2) < HALF
    even = jnp.where(first, lower, swapped(upper))
    odd = jnp.where(first, swapped(lower), upper)
    return jnp.stack([even, odd], axis=1).reshape(WIN, WIN, WIN, D)


def swapped(rows):
    shape = rows.shape
    return pltpu.roll(rows.reshape(-1, WIN, D), HALF, 1).reshape(shape)


def kept_tokens(tokens_ref, frozen_ref):
    mask = jnp.broadcast_to(frozen_ref[...][..., None], (WIN, WIN, WIN, D)) == 1
    return mask, jnp.where(mask, tokens_ref[...].astype(jnp.float32), 0.0)


def main_kernel(
    order,
    tokens_ref,
    frozen_ref,
    cot_ref,
    w_qkv_ref,
    w_proj_ref,
    gain_ref,
    restored_ref,
    total_ref,
    gain_total_ref,
    block,
    window,
    unit,
    inv_std,
    normed,
    qkv,
    d_mixed,
    d_qkv,
    mixed_t,
    back,
    grad,
    landing,
    gain_landing,
    out_send,
    out_recv,
    back_send,
    back_recv,
    reduce_send,
    reduce_recv,
    gather_send,
    gather_recv,
    gain_send,
    gain_recv,
):
    barrier = pltpu.get_barrier_semaphore()
    greeted = 0
    for octant in OCTANTS[1:]:
        for direction in (-1, 1):
            device = neighbour(octant, direction)
            pl.semaphore_signal(barrier, inc=1, device_id=device, device_id_type=MESH)
            greeted += 1
    for bits in order:
        for flips in range(1, 2 ** len(bits)):
            device = partner(bits, flips)[0]
            pl.semaphore_signal(barrier, inc=1, device_id=device, device_id_type=MESH)
            greeted += 1

    kept = split_octants(kept_tokens(tokens_ref, frozen_ref)[1])
    cot = split_octants(cot_ref[...].astype(jnp.float32))
    for k in range(8):
        target = block.at[k] if k else window.at[0:OCT]
        target[:, :D] = kept[k].astype(jnp.bfloat16)
        target[:, D:] = cot[k].astype(jnp.bfloat16)
    pl.semaphore_wait(barrier, greeted)
    unsent = []
    arriving = [None]
    for k in range(1, 8):
        device = neighbour(OCTANTS[k], -1)
        where = pl.ds(k * OCT, OCT)
        arriving.append(
            remote(block.at[k], window.at[where], out_send.at[k - 1], out_recv.at[k - 1], device)
        )

    norm_gain = gain_ref[...].reshape(1, D)
    half_rows = ROWS // 2
    for part in range(2):
        for copy in arriving[4 * part : 4 * part + 4]:
            if copy is not None:
                copy.wait_recv()
                unsent.append(copy)
        at = slice(part * half_rows, (part + 1) * half_rows)
        rows = window[at, :D].astype(jnp.float32)
        centred = rows - jnp.mean(rows, axis=-1, keepdims=True)
        inv = lax.rsqrt(jnp.mean(centred * centred, axis=-1, keepdims=True) + EPSILON)
        inv_std[at, :] = inv
        unit_part = centred * inv
        unit[at, :] = unit_part
        normed_part = (unit_part * norm_gain).astype(jnp.bfloat16)
        normed[at, :] = normed_part
        qkv[at, :] = dot(normed_part, w_qkv_ref[...]).astype(jnp.bfloat16)
        d_mixed[at, :] = dot_nt(window[at, D:], w_proj_ref[...]).astype(jnp.bfloat16)

    plan = plan_stages(order)
    sems = (reduce_send, reduce_recv, gather_send, gather_recv)
    tasks = {}

    def launch(name, task):
        tasks[name] = task
        next(task)

    def advance(*names):
        for name in names:
            if name in tasks and next(tasks[name], "done") == "done":
                del tasks[name]

    lane = lax.broadcasted_iota(jnp.int32, (ROWS, LANES), 1)
    normed_t = normed[...].T
    window_cot = window[:, D:]

    polls = {(1, 1): (0,), (2, 1): (1,), (2, 2): (0,)}

    for g in range(GROUPS):
        at = [slice(part * D + g * LANES, part * D + (g + 1) * LANES) for part in range(3)]
        queries, key_rows, values = (qkv[:, where] for where in at)
        cot_rows = d_mixed[:, at[0]]
        keys_t = key_rows.T
        values_t = values.T
        d_keys = jnp.zeros((ROWS, LANES), jnp.float32)
        d_values = jnp.zeros((ROWS, LANES), jnp.float32)
        d_queries_t = []
        mixed_parts = []
        for h in range(PER_GROUP):
            mine = (lane >= h * HDIM) & (lane < (h + 1) * HDIM)
            own_queries = jnp.where(mine, queries, jnp.zeros_like(queries))
            own_cot = jnp.where(mine, cot_rows, jnp.zeros_like(cot_rows))
            head = slice(h * HDIM, (h + 1) * HDIM)
            scores = dot_nt(key_rows, own_queries)
            top = jnp.max(scores, axis=0, keepdims=True)
            exp_terms = jnp.exp2((scores - top) * (SCALE * LOG2E))
            probs = exp_terms * (1.0 / jnp.sum(exp_terms, axis=0, keepdims=True))
            probs_low = probs.astype(jnp.bfloat16)
            mixed_parts.append(dot(values_t[head], probs_low).astype(jnp.bfloat16))
            d_values += dot(probs_low, own_cot)
            d_probs = dot_nt(values, own_cot)
            total = jnp.sum(probs * d_probs, axis=0, keepdims=True)
            d_scores = (probs * (d_probs - total) * SCALE).astype(jnp.bfloat16)
            d_queries_t.append(dot(keys_t[head], d_scores).astype(jnp.bfloat16))
            d_keys += dot(d_scores, own_queries)
            advance(*polls.get((g, h), ()))
        mixed_t[at[0], :] = jnp.concatenate(mixed_parts, axis=0)
        d_qkv[:, at[0]] = jnp.concatenate(d_queries_t, axis=0).T
        d_qkv[:, at[1]] = d_keys.astype(jnp.bfloat16)
        d_qkv[:, at[2]] = d_values.astype(jnp.bfloat16)
        start = g * (GRAD_ROWS // PARTS)
        for part in range(3):
            grad[start : start + D, :] = dot(normed_t, d_qkv[:, at[part]])
            start += D
        proj_term = dot(mixed_t[at[0], :], window_cot)
        for j in range(GROUPS):
            grad[start : start + LANES, :] = proj_term[:, j * LANES : (j + 1) * LANES]
            start += LANES
        launch(g, reduce_part(plan, g, grad, landing, total_ref, sems, unsent))

    def send_back(which):
        for k in range(1, 8):
            copy = remote(
                back.at[which, k],
                restored_ref.at[which, k],
                back_send.at[which, k - 1],
                back_recv.at[which, k - 1],
                neighbour(OCTANTS[k], 1),
            )
            unsent.append(copy)
            returning.append(copy)

    returning = []
    branch = dot(mixed_t[...].T, w_proj_ref[...]).astype(jnp.bfloat16)
    back[0] = branch.reshape(8, OCT, D)
    d_normed = dot_nt(d_qkv[...], w_qkv_ref[...])
    advance(2, 0)
    send_back(0)
    unit_rows = unit[...]
    gain_term = jnp.sum(d_normed * unit_rows, axis=0, keepdims=True)
    gain_total_ref[...] = jnp.zeros_like(gain_total_ref)
    for j in range(GROUPS):
        gain_total_ref[j : j + 1, :] = gain_term[:, j * LANES : (j + 1) * LANES]
    launch(GROUPS, reduce_gain(order, gain_total_ref, gain_landing, gain_send, gain_recv))
    scaled = d_normed * norm_gain
    d_rows = (
        inv_std[...]
        * (
            scaled
            - jnp.mean(scaled, axis=-1, keepdims=True)
            - unit_rows * jnp.mean(scaled * unit_rows, axis=-1, keepdims=True)
        )
    ).astype(jnp.bfloat16)
    back[1] = d_rows.reshape(8, OCT, D)
    send_back(1)
    for which in range(2):
        restored_ref[which, 0] = back[which, 0]
    advance(1, 0, 1, 3, 2, 0, 1, 2, 3, 1, 2)
    while tasks:
        advance(*tasks)
    for copy in returning:
        copy.wait_recv()
    for copy in unsent:
        copy.wait_send()


def finish_kernel(
    scale,
    tokens_ref,
    frozen_ref,
    cot_ref,
    restored_ref,
    total_ref,
    gain_total_ref,
    out_ref,
    tokens_grad_ref,
    qkv_grad_ref,
    proj_grad_ref,
    gain_grad_ref,
):
    wide = jnp.float32
    mask, kept = kept_tokens(tokens_ref, frozen_ref)
    branch = join_octants([restored_ref[0, k].astype(wide) for k in range(8)])
    out_ref[...] = (kept + branch).astype(jnp.bfloat16)
    d_rows = join_octants([restored_ref[1, k].astype(wide) for k in range(8)])
    both = cot_ref[...].astype(wide) + d_rows
    tokens_grad_ref[...] = jnp.where(mask, both, 0.0).astype(jnp.bfloat16)
    start = 0
    for g in range(GROUPS):
        for part in range(3):
            column = part * D + g * LANES
            qkv_grad_ref[:, column : column + LANES] = total_ref[start : start + D, :].astype(wide) * scale
            start += D
        for j in range(GROUPS):
            proj_grad_ref[g * LANES : (g + 1) * LANES, j * LANES : (j + 1) * LANES] = (
                total_ref[start : start + LANES, :].astype(wide) * scale
            )
            start += LANES
    for j in range(GROUPS):
        row = gain_total_ref[j : j + 1, :] * scale
        gain_grad_ref[j * LANES : (j + 1) * LANES] = row.reshape(LANES)


def in_vmem(count):
    return [pl.BlockSpec(memory_space=pltpu.VMEM)] * count


def local(tokens, frozen, cotangent, w_qkv, w_proj, norm_gain):
    low, wide = jnp.bfloat16, jnp.float32
    shape = jax.ShapeDtypeStruct
    order = stages()
    count = len(order)
    landing_rows = PARTS * sum(
        (2 ** len(bits) - 1) * rows for bits, rows, _ in plan_stages(order)
    )
    dma = pltpu.SemaphoreType.DMA
    restored, total, gain = pl.pallas_call(
        functools.partial(main_kernel, order),
        out_shape=(
            shape((2, 8, OCT, D), low),
            shape((GRAD_ROWS, LANES), low),
            shape((8, LANES), wide),
        ),
        in_specs=in_vmem(6),
        out_specs=tuple(in_vmem(3)),
        scratch_shapes=[
            pltpu.VMEM((8, OCT, 2 * D), low),
            pltpu.VMEM((ROWS, 2 * D), low),
            pltpu.VMEM((ROWS, D), wide),
            pltpu.VMEM((ROWS, 1), wide),
            pltpu.VMEM((ROWS, D), low),
            pltpu.VMEM((ROWS, 3 * D), low),
            pltpu.VMEM((ROWS, D), low),
            pltpu.VMEM((ROWS, 3 * D), low),
            pltpu.VMEM((D, ROWS), low),
            pltpu.VMEM((2, 8, OCT, D), low),
            pltpu.VMEM((GRAD_ROWS, LANES), wide),
            pltpu.VMEM((landing_rows, LANES), wide),
            pltpu.VMEM((count, 3, 8, LANES), wide),
            dma((7,)),
            dma((7,)),
            dma((2, 7)),
            dma((2, 7)),
            dma((PARTS, count, 3)),
            dma((PARTS, count, 3)),
            dma((PARTS, count, 3)),
            dma((PARTS, count, 3)),
            dma((count, 3)),
            dma((count, 3)),
        ],
        compiler_params=pltpu.CompilerParams(
            collective_id=0, has_side_effects=True, vmem_limit_bytes=VMEM_LIMIT
        ),
    )(tokens, frozen, cotangent, w_qkv, w_proj, norm_gain)
    everyone = ROWS
    for axis in AXES:
        everyone *= lax.axis_size(axis)
    return pl.pallas_call(
        functools.partial(finish_kernel, everyone ** (-0.5)),
        out_shape=(
            shape(tokens.shape, low),
            shape(tokens.shape, low),
            shape((D, 3 * D), wide),
            shape((D, D), wide),
            shape((D,), wide),
        ),
        in_specs=in_vmem(6),
        out_specs=tuple(in_vmem(5)),
        compiler_params=pltpu.CompilerParams(vmem_limit_bytes=VMEM_LIMIT),
    )(tokens, frozen, cotangent, restored, total, gain)


def solution(mesh):
    lattice = P(*AXES, None)
    return jax.shard_map(
        local,
        mesh=mesh,
        in_specs=(lattice, P(*AXES), lattice, P(), P(), P()),
        out_specs=(lattice, lattice, P(), P(), P()),
        check_vma=False,
    )
```

```python
import functools

import jax
import jax.numpy as jnp
from jax import lax
from jax.experimental import pallas as pl
from jax.experimental.pallas import tpu as pltpu
from jax.sharding import PartitionSpec as P

D = 384
HEADS = 12
HDIM = 32
WIN = 8
HALF = WIN // 2
OCT = HALF**3
ROWS = WIN**3
LANES = 128
PER_GROUP = LANES // HDIM
GROUPS = D // LANES
GRAD_ROWS = 4 * GROUPS * D
PARTS = 3
EPSILON = 1e-05
SCALE = HDIM ** (-0.5)
LOG2E = 1.4426950408889634
AXES = ("gx", "gy", "gz")
MESH = pl.DeviceIdType.MESH
VMEM_LIMIT = 56 * 1024 * 1024

OCTANTS = [
    (1, 1, 1),
    (1, 1, 0),
    (1, 0, 1),
    (0, 1, 1),
    (1, 0, 0),
    (0, 1, 0),
    (0, 0, 1),
    (0, 0, 0),
]


def neighbour(octant, direction):
    place = []
    for bit, axis in zip(octant, AXES, strict=True):
        size = lax.axis_size(axis)
        at = lax.axis_index(axis)
        place.append(at if bit else lax.rem(at + size + direction, size))
    return tuple(place)


def stages():
    bits = []
    for axis in ("gy", "gz", "gx"):
        step = 1
        while step < lax.axis_size(axis):
            bits.append((axis, step))
            step *= 2
    return [bits[:1]] + [bits[i : i + 2] for i in range(1, len(bits), 2)]


def my_bit(axis, step):
    return lax.rem(lax.axis_index(axis) // step, 2)


def partner(bits, flips):
    place = {axis: lax.axis_index(axis) for axis in AXES}
    digit = 0
    for i, (axis, step) in enumerate(bits):
        bit = my_bit(axis, step)
        if flips >> i & 1:
            place[axis] = place[axis] + step * (1 - 2 * bit)
            bit = 1 - bit
        digit = digit + bit * 2**i
    return tuple(place[axis] for axis in AXES), digit


def plan_stages(order):
    plan, held = [], GRAD_ROWS // PARTS
    for bits in order:
        count = 2 ** len(bits)
        divided = held % (16 * count) == 0
        if divided:
            held //= count
        plan.append((bits, held, divided))
    return plan


def tree_sum(terms):
    while len(terms) > 1:
        terms = [a + b for a, b in zip(terms[::2], terms[1::2], strict=True)]
    return terms[0]


def remote(src, dst, send_sem, recv_sem, device):
    copy = pltpu.make_async_remote_copy(
        src_ref=src,
        dst_ref=dst,
        send_sem=send_sem,
        recv_sem=recv_sem,
        device_id=device,
        device_id_type=MESH,
    )
    copy.start()
    return copy


def reduce_part(plan, p, grad, landing, total_ref, sems, unsent):
    reduce_send, reduce_recv, gather_send, gather_recv = sems
    low = p * (GRAD_ROWS // PARTS)
    offset = p * (landing.shape[0] // PARTS)
    for s, (bits, rows, divided) in enumerate(plan):
        copies = []
        for flips in range(1, 2 ** len(bits)):
            device, digit = partner(bits, flips)
            start = pl.multiple_of(low + digit * rows, 16) if divided else low
            copies.append(
                remote(
                    grad.at[pl.ds(start, rows)],
                    landing.at[pl.ds(offset + (flips - 1) * rows, rows)],
                    reduce_send.at[p, s, flips - 1],
                    reduce_recv.at[p, s, flips - 1],
                    device,
                )
            )
        yield
        for copy in copies:
            copy.wait_recv()
            if divided:
                unsent.append(copy)
            else:
                copy.wait_send()
        if divided:
            low = pl.multiple_of(low + partner(bits, 0)[1] * rows, 16)
        where = pl.ds(low, rows)
        terms = [grad[where, :]]
        for _ in copies:
            terms.append(landing[offset : offset + rows, :])
            offset += rows
        grad[where, :] = tree_sum(terms)
    where = pl.ds(low, plan[-1][1])
    total_ref[where, :] = grad[where, :].astype(jnp.bfloat16)
    for s, (bits, rows, divided) in reversed(list(enumerate(plan))):
        if not divided:
            continue
        copies = []
        where = pl.ds(low, rows)
        for flips in range(1, 2 ** len(bits)):
            copies.append(
                remote(
                    total_ref.at[where],
                    total_ref.at[where],
                    gather_send.at[p, s, flips - 1],
                    gather_recv.at[p, s, flips - 1],
                    partner(bits, flips)[0],
                )
            )
        yield
        for copy in copies:
            copy.wait_recv()
            unsent.append(copy)
        low = pl.multiple_of(low - partner(bits, 0)[1] * rows, 16)


def reduce_gain(order, gain_ref, landing, send_sem, recv_sem):
    for s, bits in enumerate(order):
        copies = []
        for flips in range(1, 2 ** len(bits)):
            copies.append(
                remote(
                    gain_ref,
                    landing.at[s, flips - 1],
                    send_sem.at[s, flips - 1],
                    recv_sem.at[s, flips - 1],
                    partner(bits, flips)[0],
                )
            )
        yield
        for copy in copies:
            copy.wait()
        terms = [gain_ref[...]] + [landing[s, i] for i in range(len(copies))]
        gain_ref[...] = tree_sum(terms)


def dot(a, b):
    return lax.dot_general(a, b, (((1,), (0,)), ((), ())), preferred_element_type=jnp.float32)


def dot_nt(a, b):
    return lax.dot_general(a, b, (((1,), (1,)), ((), ())), preferred_element_type=jnp.float32)


def split_octants(block):
    pairs = block.reshape(HALF, 2, WIN, WIN, D)
    even, odd = pairs[:, 0], pairs[:, 1]
    first = lax.broadcasted_iota(jnp.int32, even.shape, 2) < HALF
    halves = [
        jnp.where(first, even, swapped(odd)),
        jnp.where(first, swapped(even), odd),
    ]
    found = []
    for ox, oy, oz in OCTANTS:
        part = halves[oz][2 * ox : 2 * ox + 2, HALF * oy : HALF * oy + HALF]
        found.append(part.reshape(OCT, D))
    return found


def join_octants(octants):
    parts = dict(zip(OCTANTS, octants, strict=True))
    halves = []
    for oz in range(2):
        rows = []
        for ox in range(2):
            both = [parts[ox, oy, oz].reshape(2, HALF, WIN, D) for oy in range(2)]
            rows.append(jnp.concatenate(both, axis=1))
        halves.append(jnp.concatenate(rows, axis=0))
    lower, upper = halves
    first = lax.broadcasted_iota(jnp.int32, lower.shape, 2) < HALF
    even = jnp.where(first, lower, swapped(upper))
    odd = jnp.where(first, swapped(lower), upper)
    return jnp.stack([even, odd], axis=1).reshape(WIN, WIN, WIN, D)


def swapped(rows):
    shape = rows.shape
    return pltpu.roll(rows.reshape(-1, WIN, D), HALF, 1).reshape(shape)


def kept_tokens(tokens_ref, frozen_ref):
    mask = jnp.broadcast_to(frozen_ref[...][..., None], (WIN, WIN, WIN, D)) == 1
    return mask, jnp.where(mask, tokens_ref[...].astype(jnp.float32), 0.0)


def main_kernel(
    order,
    tokens_ref,
    frozen_ref,
    cot_ref,
    w_qkv_ref,
    w_proj_ref,
    gain_ref,
    restored_ref,
    total_ref,
    gain_total_ref,
    block,
    window,
    unit,
    inv_std,
    normed,
    qkv,
    d_mixed,
    d_qkv,
    mixed_t,
    probs,
    back,
    grad,
    landing,
    gain_landing,
    out_send,
    out_recv,
    back_send,
    back_recv,
    reduce_send,
    reduce_recv,
    gather_send,
    gather_recv,
    gain_send,
    gain_recv,
):
    barrier = pltpu.get_barrier_semaphore()
    greeted = 0
    for octant in OCTANTS[1:]:
        for direction in (-1, 1):
            device = neighbour(octant, direction)
            pl.semaphore_signal(barrier, inc=1, device_id=device, device_id_type=MESH)
            greeted += 1
    for bits in order:
        for flips in range(1, 2 ** len(bits)):
            device = partner(bits, flips)[0]
            pl.semaphore_signal(barrier, inc=1, device_id=device, device_id_type=MESH)
            greeted += 1

    kept = split_octants(kept_tokens(tokens_ref, frozen_ref)[1])
    cot = split_octants(cot_ref[...].astype(jnp.float32))
    for k in range(8):
        target = block.at[k] if k else window.at[0:OCT]
        target[:, :D] = kept[k].astype(jnp.bfloat16)
        target[:, D:] = cot[k].astype(jnp.bfloat16)
    pl.semaphore_wait(barrier, greeted)
    unsent = []
    arriving = [None]
    for k in range(1, 8):
        device = neighbour(OCTANTS[k], -1)
        where = pl.ds(k * OCT, OCT)
        arriving.append(
            remote(block.at[k], window.at[where], out_send.at[k - 1], out_recv.at[k - 1], device)
        )

    norm_gain = gain_ref[...].reshape(1, D)
    half_rows = ROWS // 2
    for part in range(2):
        for copy in arriving[4 * part : 4 * part + 4]:
            if copy is not None:
                copy.wait_recv()
                unsent.append(copy)
        at = slice(part * half_rows, (part + 1) * half_rows)
        rows = window[at, :D].astype(jnp.float32)
        centred = rows - jnp.mean(rows, axis=-1, keepdims=True)
        inv = lax.rsqrt(jnp.mean(centred * centred, axis=-1, keepdims=True) + EPSILON)
        inv_std[at, :] = inv
        unit_part = centred * inv
        unit[at, :] = unit_part
        normed_part = (unit_part * norm_gain).astype(jnp.bfloat16)
        normed[at, :] = normed_part
        qkv[at, :] = dot(normed_part, w_qkv_ref[...]).astype(jnp.bfloat16)
        d_mixed[at, :] = dot_nt(window[at, D:], w_proj_ref[...]).astype(jnp.bfloat16)

    plan = plan_stages(order)
    sems = (reduce_send, reduce_recv, gather_send, gather_recv)
    tasks = {}

    def launch(name, task):
        tasks[name] = task
        next(task)

    def advance(*names):
        for name in names:
            if name in tasks and next(tasks[name], "done") == "done":
                del tasks[name]

    lane = lax.broadcasted_iota(jnp.int32, (ROWS, LANES), 1)
    normed_t = normed[...].T
    window_cot = window[:, D:]

    def columns(part, g):
        return slice(part * D + g * LANES, part * D + (g + 1) * LANES)

    def own_lanes(rows, h):
        mine = (lane >= h * HDIM) & (lane < (h + 1) * HDIM)
        return jnp.where(mine, rows, jnp.zeros_like(rows))

    for g in range(GROUPS):
        queries, key_rows, values = (qkv[:, columns(part, g)] for part in range(3))
        values_t = values.T
        mixed_parts = []
        for h in range(PER_GROUP):
            scores = dot_nt(key_rows, own_lanes(queries, h))
            top = jnp.max(scores, axis=0, keepdims=True)
            exp_terms = jnp.exp2((scores - top) * (SCALE * LOG2E))
            head_probs = exp_terms * (1.0 / jnp.sum(exp_terms, axis=0, keepdims=True))
            probs[g * PER_GROUP + h] = head_probs
            head = slice(h * HDIM, (h + 1) * HDIM)
            mixed_parts.append(
                dot(values_t[head], head_probs.astype(jnp.bfloat16)).astype(jnp.bfloat16)
            )
        mixed_t[columns(0, g), :] = jnp.concatenate(mixed_parts, axis=0)

    returning = []

    def send_back(which):
        for k in range(1, 8):
            copy = remote(
                back.at[which, k],
                restored_ref.at[which, k],
                back_send.at[which, k - 1],
                back_recv.at[which, k - 1],
                neighbour(OCTANTS[k], 1),
            )
            unsent.append(copy)
            returning.append(copy)

    branch = dot(mixed_t[...].T, w_proj_ref[...]).astype(jnp.bfloat16)
    back[0] = branch.reshape(8, OCT, D)
    send_back(0)

    polls = {(1, 2): (0,), (2, 2): (1,)}

    for g in range(GROUPS):
        queries, key_rows, values = (qkv[:, columns(part, g)] for part in range(3))
        cot_rows = d_mixed[:, columns(0, g)]
        keys_t = key_rows.T
        d_keys = jnp.zeros((ROWS, LANES), jnp.float32)
        d_values = jnp.zeros((ROWS, LANES), jnp.float32)
        d_queries_t = []
        for h in range(PER_GROUP):
            own_queries = own_lanes(queries, h)
            own_cot = own_lanes(cot_rows, h)
            head = slice(h * HDIM, (h + 1) * HDIM)
            head_probs = probs[g * PER_GROUP + h]
            d_values += dot(head_probs.astype(jnp.bfloat16), own_cot)
            d_probs = dot_nt(values, own_cot)
            total = jnp.sum(head_probs * d_probs, axis=0, keepdims=True)
            d_scores = (head_probs * (d_probs - total) * SCALE).astype(jnp.bfloat16)
            d_queries_t.append(dot(keys_t[head], d_scores).astype(jnp.bfloat16))
            d_keys += dot(d_scores, own_queries)
            advance(*polls.get((g, h), ()))
        d_qkv[:, columns(0, g)] = jnp.concatenate(d_queries_t, axis=0).T
        d_qkv[:, columns(1, g)] = d_keys.astype(jnp.bfloat16)
        d_qkv[:, columns(2, g)] = d_values.astype(jnp.bfloat16)
        start = g * (GRAD_ROWS // PARTS)
        for part in range(3):
            grad[start : start + D, :] = dot(normed_t, d_qkv[:, columns(part, g)])
            start += D
        proj_term = dot(mixed_t[columns(0, g), :], window_cot)
        for j in range(GROUPS):
            grad[start : start + LANES, :] = proj_term[:, j * LANES : (j + 1) * LANES]
            start += LANES
        launch(g, reduce_part(plan, g, grad, landing, total_ref, sems, unsent))

    d_normed = dot_nt(d_qkv[...], w_qkv_ref[...])
    advance(2)
    unit_rows = unit[...]
    gain_term = jnp.sum(d_normed * unit_rows, axis=0, keepdims=True)
    gain_total_ref[...] = jnp.zeros_like(gain_total_ref)
    for j in range(GROUPS):
        gain_total_ref[j : j + 1, :] = gain_term[:, j * LANES : (j + 1) * LANES]
    launch(GROUPS, reduce_gain(order, gain_total_ref, gain_landing, gain_send, gain_recv))
    scaled = d_normed * norm_gain
    d_rows = (
        inv_std[...]
        * (
            scaled
            - jnp.mean(scaled, axis=-1, keepdims=True)
            - unit_rows * jnp.mean(scaled * unit_rows, axis=-1, keepdims=True)
        )
    ).astype(jnp.bfloat16)
    back[1] = d_rows.reshape(8, OCT, D)
    send_back(1)
    for which in range(2):
        restored_ref[which, 0] = back[which, 0]
    advance(0, 1, 3, 0, 2, 1, 3, 0, 2, 1, 0, 2, 1, 3, 2)
    while tasks:
        advance(*tasks)
    for copy in returning:
        copy.wait_recv()
    for copy in unsent:
        copy.wait_send()


def finish_kernel(
    scale,
    tokens_ref,
    frozen_ref,
    cot_ref,
    restored_ref,
    total_ref,
    gain_total_ref,
    out_ref,
    tokens_grad_ref,
    qkv_grad_ref,
    proj_grad_ref,
    gain_grad_ref,
):
    wide = jnp.float32
    mask, kept = kept_tokens(tokens_ref, frozen_ref)
    branch = join_octants([restored_ref[0, k].astype(wide) for k in range(8)])
    out_ref[...] = (kept + branch).astype(jnp.bfloat16)
    d_rows = join_octants([restored_ref[1, k].astype(wide) for k in range(8)])
    both = cot_ref[...].astype(wide) + d_rows
    tokens_grad_ref[...] = jnp.where(mask, both, 0.0).astype(jnp.bfloat16)
    start = 0
    for g in range(GROUPS):
        for part in range(3):
            column = part * D + g * LANES
            qkv_grad_ref[:, column : column + LANES] = total_ref[start : start + D, :].astype(wide) * scale
            start += D
        for j in range(GROUPS):
            proj_grad_ref[g * LANES : (g + 1) * LANES, j * LANES : (j + 1) * LANES] = (
                total_ref[start : start + LANES, :].astype(wide) * scale
            )
            start += LANES
    for j in range(GROUPS):
        row = gain_total_ref[j : j + 1, :] * scale
        gain_grad_ref[j * LANES : (j + 1) * LANES] = row.reshape(LANES)


def in_vmem(count):
    return [pl.BlockSpec(memory_space=pltpu.VMEM)] * count


def local(tokens, frozen, cotangent, w_qkv, w_proj, norm_gain):
    low, wide = jnp.bfloat16, jnp.float32
    shape = jax.ShapeDtypeStruct
    order = stages()
    count = len(order)
    landing_rows = PARTS * sum(
        (2 ** len(bits) - 1) * rows for bits, rows, _ in plan_stages(order)
    )
    dma = pltpu.SemaphoreType.DMA
    restored, total, gain = pl.pallas_call(
        functools.partial(main_kernel, order),
        out_shape=(
            shape((2, 8, OCT, D), low),
            shape((GRAD_ROWS, LANES), low),
            shape((8, LANES), wide),
        ),
        in_specs=in_vmem(6),
        out_specs=tuple(in_vmem(3)),
        scratch_shapes=[
            pltpu.VMEM((8, OCT, 2 * D), low),
            pltpu.VMEM((ROWS, 2 * D), low),
            pltpu.VMEM((ROWS, D), wide),
            pltpu.VMEM((ROWS, 1), wide),
            pltpu.VMEM((ROWS, D), low),
            pltpu.VMEM((ROWS, 3 * D), low),
            pltpu.VMEM((ROWS, D), low),
            pltpu.VMEM((ROWS, 3 * D), low),
            pltpu.VMEM((D, ROWS), low),
            pltpu.VMEM((HEADS, ROWS, ROWS), wide),
            pltpu.VMEM((2, 8, OCT, D), low),
            pltpu.VMEM((GRAD_ROWS, LANES), wide),
            pltpu.VMEM((landing_rows, LANES), wide),
            pltpu.VMEM((count, 3, 8, LANES), wide),
            dma((7,)),
            dma((7,)),
            dma((2, 7)),
            dma((2, 7)),
            dma((PARTS, count, 3)),
            dma((PARTS, count, 3)),
            dma((PARTS, count, 3)),
            dma((PARTS, count, 3)),
            dma((count, 3)),
            dma((count, 3)),
        ],
        compiler_params=pltpu.CompilerParams(
            collective_id=0, has_side_effects=True, vmem_limit_bytes=VMEM_LIMIT
        ),
    )(tokens, frozen, cotangent, w_qkv, w_proj, norm_gain)
    everyone = ROWS
    for axis in AXES:
        everyone *= lax.axis_size(axis)
    return pl.pallas_call(
        functools.partial(finish_kernel, everyone ** (-0.5)),
        out_shape=(
            shape(tokens.shape, low),
            shape(tokens.shape, low),
            shape((D, 3 * D), wide),
            shape((D, D), wide),
            shape((D,), wide),
        ),
        in_specs=in_vmem(6),
        out_specs=tuple(in_vmem(5)),
        compiler_params=pltpu.CompilerParams(vmem_limit_bytes=VMEM_LIMIT),
    )(tokens, frozen, cotangent, restored, total, gain)


def solution(mesh):
    lattice = P(*AXES, None)
    return jax.shard_map(
        local,
        mesh=mesh,
        in_specs=(lattice, P(*AXES), lattice, P(), P(), P()),
        out_specs=(lattice, lattice, P(), P(), P()),
        check_vma=False,
    )
```
